32 devices in a mesh: dp: 8 (over z, x), tensor: 4 (over y, core).
Axes of the slice: x: 2, y: 2, z: 4, core: 2. Of those that a mesh axis runs over, the one named last changes fastest.
Arguments:
- grads_out: bfloat16 [256, 28672], P('dp'), may hold values from -6 to 6
- inputs: bfloat16 [256, 8192], P('dp'), may hold values from -6 to 6
- basis_out: bfloat16 [28672, 14336], P('dp', 'tensor'), may hold values from -0.03125 to 0.03125
- basis_in: bfloat16 [8192, 4096], P('tensor', 'dp'), may hold values from -0.0625 to 0.0625
- lengths: int32 [8], P('dp'), may hold values from 1 to 32, as said below
Outputs:
- corrections: float32 [14336, 4096], P('tensor', 'dp')
The draws below stay inside these ranges and needn't reach their ends.
Inputs may be any that keep to these rules, and one draw needn't show every extreme that they name: `lengths`: every sequence has at least one live token, and some sequence has all 32 slots live.
All inputs are finite; a program needn't handle non-finite values.
Results may differ from the reference program's by a relative error of at most 0.0026.
Values may be sent and summed in bfloat16 or wider, within the bound.
A program may use at most 128 MiB of HBM per device.

```python
import jax
import jax.numpy as jnp
from jax import lax

D = 8192
FF = 28672
FW = 14336
DW = 4096
LEN = 32
SEQS = 8
TOKENS = 256


def draw_lengths(key, part):
    inner = jax.random.fold_in(key, 11)
    first_key, second_key = jax.random.split(inner)
    base = jax.random.randint(first_key, (SEQS,), 1, LEN + 1)
    chosen = jax.random.randint(second_key, (), 0, SEQS)
    return jnp.where(jnp.arange(SEQS) == chosen, LEN, base).astype(jnp.int32)


def level_of(key, dims, cuts, smallest, high):
    loudness = 1.0
    for dim, shards_of in cuts:
        steps = jax.random.uniform(jax.random.fold_in(jax.random.fold_in(key, 6), dim), (shards_of,), jnp.float32, smallest / len(cuts), high / len(cuts))
        loudness = loudness * jnp.repeat(jnp.exp(steps), dims[dim] // shards_of).reshape((-1,) + (1,) * (len(dims) - 1 - dim))
    return loudness


def normal_values(rng, extent, width, most, shards=(), kind=jnp.bfloat16):
    result = width * jax.random.normal(rng, extent, jnp.float32)
    if shards:
        result = result * level_of(rng, extent, shards, -0.22, 0.18)
    return jnp.clip(result, -most, most).astype(kind)


def setup_inputs(seed: int = 0) -> dict:
    seeds = jax.random.split(jax.random.key(seed), 6)
    grads_out = normal_values(seeds[0], (TOKENS, FF), 1.0, 6.0, ((0, 8),))
    inputs = normal_values(seeds[1], (TOKENS, D), 1.0, 6.0, ((0, 8),))
    basis_out = normal_values(seeds[2], (FF, FW), FF ** -0.5, 0.03125, ((0, 8), (1, 4)))
    basis_in = normal_values(seeds[3], (D, DW), D ** -0.5, 0.0625, ((0, 4), (1, 8)))
    lengths = draw_lengths(jax.random.fold_in(seeds[5], 71), 0)
    return dict(grads_out=grads_out, inputs=inputs, basis_out=basis_out, basis_in=basis_in, lengths=lengths)


def reference(grads_out, inputs, basis_out, basis_in, lengths):
    positions = jnp.arange(LEN).astype(jnp.int32)
    live = (positions[None, :] < lengths[:, None]).reshape(-1)
    masked = jnp.where(live[:, None], grads_out, jnp.zeros_like(grads_out))
    rotated = jnp.dot(masked, basis_out, preferred_element_type=jnp.float32).astype(jnp.bfloat16)
    panel = jnp.dot(inputs, basis_in, preferred_element_type=jnp.float32).astype(jnp.bfloat16)
    rotated_seq = rotated.reshape(SEQS, LEN, FW)
    panel_seq = panel.reshape(SEQS, LEN, DW)

    def accumulate(total, pair):
        left_factor, right_factor = pair
        sample_case = jnp.dot(left_factor.T, right_factor, preferred_element_type=jnp.float32)
        return total + sample_case * sample_case, None

    total, unused = lax.scan(accumulate, jnp.zeros((FW, DW), jnp.float32), (rotated_seq, panel_seq))
    return total / TOKENS
```

```python
import functools

import jax
import jax.numpy as jnp
from jax import lax
from jax.experimental import pallas as pl
from jax.experimental.pallas import tpu as pltpu
from jax.sharding import PartitionSpec as P

MESH = pl.DeviceIdType.MESH
BF16 = jnp.bfloat16
F32 = jnp.float32


def ring_to_dp(q, n):
    return jnp.where(q < n // 2, 2 * q, 2 * (n - 1 - q) + 1)


def exchange_kernel(
    n, tn, nc, share_y,
    grads, inputs, basis_out, basis_in, lengths,
    rotated_out, panel_out,
    gathered, basis, slab, basis_small, partial, early_send, early_recv, late_send, late_recv, rotated,
    panel_part, panel_recv, panel,
    a_send, a_recv, fy_send, fy_recv, fc_send, fc_recv, fd_send, fd_recv,
    in_send, in_recv, rs_ssem, rs_rsem, ag_ssem, ag_rsem,
    pr_send, pr_recv, pg_send, pg_recv, local_sem,
):
    d = lax.axis_index("dp")
    t = lax.axis_index("tensor")
    half = n // 2
    length = grads.shape[0]
    hl = length // 2
    width = gathered.shape[1]
    chunk = partial.shape[1] // nc
    slab_width = slab.shape[1]
    z, x = d // 2, d % 2
    pos = jnp.where(x == 0, z, n - 1 - z)
    core = t % 2
    up = t // 2

    def at_ring(offset):
        return ring_to_dp(lax.rem(pos + offset + 2 * n, n), n)

    def rows_of(index, extra=0, size=length):
        return pl.ds(pl.multiple_of(index * length + extra, hl), size)

    basis_copies = []
    pieces = 4
    step_rows = width // pieces
    for i in range(pieces):
        r = pl.ds(i * step_rows, step_rows)
        basis_copies.append(pltpu.make_async_copy(basis_out.at[r], basis.at[r], local_sem.at[i]))
    own_cols = pl.ds(pl.multiple_of(d * width, 128), width)
    own_grads = pltpu.make_async_copy(grads.at[:, own_cols], gathered.at[rows_of(d)], local_sem.at[pieces])
    slab_cols = pl.ds(pl.multiple_of(t * slab_width, 128), slab_width)
    own_slab = pltpu.make_async_copy(inputs.at[:, slab_cols], slab.at[rows_of(d)], local_sem.at[pieces + 1])
    own_small = pltpu.make_async_copy(basis_in, basis_small, local_sem.at[pieces + 2])
    own_grads.start()
    own_slab.start()
    for c in basis_copies:
        c.start()
    own_small.start()

    barrier = pltpu.get_barrier_semaphore()
    for k in range(1, n):
        pl.semaphore_signal(barrier, inc=1, device_id=(lax.rem(d + k, n), t), device_id_type=MESH)
    for k in range(1, tn):
        pl.semaphore_signal(barrier, inc=1, device_id=(d, lax.rem(t + k, tn)), device_id_type=MESH)
    pl.semaphore_wait(barrier, n - 1 + tn - 1)

    piece = width // share_y
    my_y = up if share_y == 2 else 0
    row_extra = core * hl
    mine = pl.ds(pl.multiple_of(my_y * piece, 128), piece)
    other = pl.ds(pl.multiple_of((1 - my_y) * piece, 128), piece)

    def a_copy(k, source, target):
        cols = pl.ds(pl.multiple_of(target * width + my_y * piece, 128), piece)
        return pltpu.make_async_remote_copy(
            src_ref=grads.at[pl.ds(pl.multiple_of(row_extra, hl), hl), cols],
            dst_ref=gathered.at[rows_of(source, row_extra, hl), mine],
            send_sem=a_send.at[k], recv_sem=a_recv.at[k],
            device_id=(target, t), device_id_type=MESH)

    def forward(k, extra, cols, ssem, rsem, target_t):
        ref = gathered.at[rows_of(lax.rem(d - k + n, n), extra, hl), cols]
        return pltpu.make_async_remote_copy(
            src_ref=ref, dst_ref=ref, send_sem=ssem.at[k], recv_sem=rsem.at[k],
            device_id=(d, target_t), device_id_type=MESH)

    partner = up * 2 + (1 - core)
    across = lax.rem(t + 2, tn)
    order = []
    for k in range(1, n // 2 + 1):
        order.append(k)
        if n - k != k:
            order.append(n - k)
    order = order[::-1]
    for k in order:
        a_copy(k, d, lax.rem(d + k, n)).start()

    def in_copy(direction, s, receiving):
        sign = 1 if direction == 0 else -1
        q = (-sign) * (s + 1 if receiving else s)
        last = s == half - 1
        extra = direction * hl if last else 0
        ref = slab.at[rows_of(at_ring(q), extra, hl if last else length)]
        return pltpu.make_async_remote_copy(
            src_ref=ref, dst_ref=ref, send_sem=in_send.at[direction, s], recv_sem=in_recv.at[direction, s],
            device_id=(at_ring(sign), t), device_id_type=MESH)

    own_slab.wait()
    for direction in range(2):
        in_copy(direction, 0, False).start()

    for k in order:
        a_copy(k, lax.rem(d - k + n, n), d).wait_recv()
        if share_y == 2:
            forward(k, row_extra, mine, fy_send, fy_recv, across).start()
        forward(k, row_extra, mine, fc_send, fc_recv, partner).start()
    if share_y == 2:
        for k in order:
            forward(k, row_extra, other, fy_send, fy_recv, across).wait_recv()
            forward(k, row_extra, other, fd_send, fd_recv, partner).start()
    there = hl - row_extra
    for k in order:
        forward(k, there, mine, fc_send, fc_recv, partner).wait_recv()
        if share_y == 2:
            forward(k, there, other, fd_send, fd_recv, partner).wait_recv()
    own_grads.wait()
    for c in basis_copies:
        c.wait()

    early = early_send.shape[1]

    def rs_send(direction, s, c):
        return early_send.at[direction, s, c] if s < early else late_send.at[direction, s - early, c]

    def rs_recv(direction, s, c):
        return early_recv.at[direction, s, c] if s < early else late_recv.at[direction, s - early, c]

    def rs_copy(direction, s, c):
        size = hl if s == 0 else length
        r = pl.ds(0, size)
        sign = 1 if direction == 0 else -1
        return pltpu.make_async_remote_copy(
            src_ref=rs_send(direction, s, c).at[r], dst_ref=rs_recv(direction, s, c).at[r],
            send_sem=rs_ssem.at[direction, s, c], recv_sem=rs_rsem.at[direction, s, c],
            device_id=(at_ring(sign), t), device_id_type=MESH)

    def cols_of(c):
        return pl.ds(pl.multiple_of(c * chunk, 128), chunk)

    def rotate(c):
        cols = cols_of(c)
        partial[:, cols] = jnp.dot(gathered[...], basis[:, cols], preferred_element_type=F32)
        target = at_ring(half)
        for direction in range(2):
            early_send[direction, 0, c, :hl] = partial[rows_of(target, direction * hl, hl), cols].astype(BF16)
            rs_copy(direction, 0, c).start()

    done = 0
    for s in range(1, half):
        until = max(done, min(nc, (2 * s) if nc > 2 else 1))
        if until > done:
            lax.fori_loop(done, until, lambda c, u: (rotate(c), u)[1], 0)
        done = until
        for direction in range(2):
            in_copy(direction, s - 1, True).wait_recv()
            in_copy(direction, s, False).start()
    if done < nc:
        lax.fori_loop(done, nc, lambda c, u: (rotate(c), u)[1], 0)

    for direction in range(2):
        in_copy(direction, half - 1, True).wait_recv()
    own_small.wait()
    panel_part[...] = jnp.dot(slab[...], basis_small[...], preferred_element_type=F32)
    share = panel_part.shape[0] // tn

    def share_rows(index):
        return pl.ds(pl.multiple_of(index * share, 16), share)

    def pr_copy(k):
        target = lax.rem(t + k, tn)
        return pltpu.make_async_remote_copy(
            src_ref=panel_part.at[share_rows(target)], dst_ref=panel_recv.at[k],
            send_sem=pr_send.at[k], recv_sem=pr_recv.at[k],
            device_id=(d, target), device_id_type=MESH)

    def pg_copy(k, source):
        ref = panel.at[share_rows(source)]
        return pltpu.make_async_remote_copy(
            src_ref=ref, dst_ref=ref, send_sem=pg_send.at[k], recv_sem=pg_recv.at[k],
            device_id=(d, lax.rem(t + k, tn)), device_id_type=MESH)

    for k in range(1, tn):
        pr_copy(k).start()

    for s in range(1, half):
        def reduce_step(c, u, s=s):
            cols = cols_of(c)
            for direction in range(2):
                sign = 1 if direction == 0 else -1
                target = at_ring(sign * (half - s))
                rs_copy(direction, s - 1, c).wait_recv()
                if s == 1:
                    near = slice(0, hl) if direction == 0 else slice(hl, length)
                    far = slice(hl, length) if direction == 0 else slice(0, hl)
                    near_at, far_at = direction * hl, (1 - direction) * hl
                    early_send[direction, s, c, near] = (
                        partial[rows_of(target, near_at, hl), cols]
                        + early_recv[direction, 0, c, :hl].astype(F32)).astype(BF16)
                    early_send[direction, s, c, far] = partial[rows_of(target, far_at, hl), cols].astype(BF16)
                else:
                    late_send[direction, s - early, c] = (
                        partial[rows_of(target), cols] + rs_recv(direction, s - 1, c)[...].astype(F32))
                rs_copy(direction, s, c).start()
            return u
        lax.fori_loop(0, nc, reduce_step, 0)
        if s == 1:
            total = panel_part[share_rows(t)]
            for k in range(1, tn):
                pr_copy(k).wait_recv()
                total = total + panel_recv[k]
            panel[share_rows(t)] = total.astype(BF16)
            for k in range(1, tn):
                pg_copy(k, t).start()

    def ag_copy(direction, s, c, receiving):
        sign = 1 if direction == 0 else -1
        q = (-sign) * (s + 1 if receiving else s)
        last = s == half - 1
        extra = direction * hl if last else 0
        ref = rotated.at[c, rows_of(at_ring(q), extra, hl if last else length)]
        return pltpu.make_async_remote_copy(
            src_ref=ref, dst_ref=ref, send_sem=ag_ssem.at[direction, s, c], recv_sem=ag_rsem.at[direction, s, c],
            device_id=(at_ring(sign), t), device_id_type=MESH)

    live = lax.broadcasted_iota(jnp.int32, (length, chunk), 0) < lengths[0]

    def finish(c, u):
        cols = cols_of(c)
        for direction in range(2):
            rs_copy(direction, half - 1, c).wait_recv()
        total = partial[rows_of(d), cols]
        total = total + rs_recv(0, half - 1, c)[...] + rs_recv(1, half - 1, c)[...]
        rotated[c, rows_of(d)] = jnp.where(live, total, 0.0).astype(BF16)
        for direction in range(2):
            ag_copy(direction, 0, c, False).start()
        return u
    lax.fori_loop(0, nc, finish, 0)
    for s in range(1, half):
        def pass_on(c, u, s=s):
            for direction in range(2):
                ag_copy(direction, s - 1, c, True).wait_recv()
                ag_copy(direction, s, c, False).start()
            return u
        lax.fori_loop(0, nc, pass_on, 0)

    for k in range(1, tn):
        pg_copy(k, lax.rem(t - k + tn, tn)).wait_recv()
    panel_store = pltpu.make_async_copy(panel, panel_out, local_sem.at[pieces + 3])
    panel_store.start()

    def last_step(c, u):
        for direction in range(2):
            ag_copy(direction, half - 1, c, True).wait_recv()
        return u
    lax.fori_loop(0, nc, last_step, 0)
    rotated_store = pltpu.make_async_copy(rotated, rotated_out, local_sem.at[pieces + 4])
    rotated_store.start()

    for k in order:
        a_copy(k, d, lax.rem(d + k, n)).wait_send()
        forward(k, row_extra, mine, fc_send, fc_recv, partner).wait_send()
        if share_y == 2:
            forward(k, row_extra, mine, fy_send, fy_recv, across).wait_send()
            forward(k, row_extra, other, fd_send, fd_recv, partner).wait_send()
    for s in range(half):
        for direction in range(2):
            in_copy(direction, s, False).wait_send()

        def sent(c, u, s=s):
            for direction in range(2):
                rs_copy(direction, s, c).wait_send()
                ag_copy(direction, s, c, False).wait_send()
            return u
        lax.fori_loop(0, nc, sent, 0)
    for k in range(1, tn):
        pr_copy(k).wait_send()
        pg_copy(k, t).wait_send()
    panel_store.wait()
    rotated_store.wait()


def square_kernel(sequences, length, scale, rotated, panel, out):
    total = None
    for s in range(sequences):
        r = slice(s * length, (s + 1) * length)
        example = lax.dot_general(
            rotated[0, r, :], panel[r, :], (((0,), (0,)), ((), ())), preferred_element_type=F32)
        total = example * example if total is None else total + example * example
    out[...] = total * scale


def pick_chunk(width):
    for size in (512, 256, 128):
        if width % size == 0:
            return size
    return width


def per_device(grads_out, inputs, basis_out, basis_in, lengths):
    n, tn = lax.axis_size("dp"), lax.axis_size("tensor")
    length = grads_out.shape[0]
    rows = n * length
    width, columns = basis_out.shape
    slab_width, panel_width = basis_in.shape
    half = n // 2
    chunk = pick_chunk(columns) if n <= 8 else columns
    nc = columns // chunk
    share_y = 2 if tn == 4 and width % 256 == 0 else 1
    dma = pltpu.SemaphoreType.DMA
    anywhere = pl.BlockSpec(memory_space=pl.ANY)
    flops = 2 * rows * width * columns + 2 * rows * slab_width * panel_width
    rotated, panel = pl.pallas_call(
        functools.partial(exchange_kernel, n, tn, nc, share_y),
        out_shape=(
            jax.ShapeDtypeStruct((nc, rows, chunk), BF16),
            jax.ShapeDtypeStruct((rows, panel_width), BF16),
        ),
        in_specs=[anywhere] * 4 + [pl.BlockSpec(memory_space=pltpu.SMEM)],
        out_specs=(anywhere, anywhere),
        scratch_shapes=[
            pltpu.VMEM((rows, width), BF16),
            pltpu.VMEM((width, columns), BF16),
            pltpu.VMEM((rows, slab_width), BF16),
            pltpu.VMEM((slab_width, panel_width), BF16),
            pltpu.VMEM((rows, columns), F32),
            pltpu.VMEM((2, 2, nc, length, chunk), BF16),
            pltpu.VMEM((2, 2, nc, length, chunk), BF16),
            pltpu.VMEM((2, half - 2, nc, length, chunk), F32),
            pltpu.VMEM((2, half - 2, nc, length, chunk), F32),
            pltpu.VMEM((nc, rows, chunk), BF16),
            pltpu.VMEM((rows, panel_width), F32),
            pltpu.VMEM((tn, rows // tn, panel_width), F32),
            pltpu.VMEM((rows, panel_width), BF16),
            dma((n,)), dma((n,)), dma((n,)), dma((n,)), dma((n,)), dma((n,)), dma((n,)), dma((n,)),
            dma((2, half)), dma((2, half)),
            dma((2, half, nc)), dma((2, half, nc)), dma((2, half, nc)), dma((2, half, nc)),
            dma((tn,)), dma((tn,)), dma((tn,)), dma((tn,)),
            dma((9,)),
        ],
        cost_estimate=pl.CostEstimate(
            flops=flops, bytes_accessed=2 * (width * columns + slab_width * panel_width), transcendentals=0),
        compiler_params=pltpu.CompilerParams(
            collective_id=0, has_side_effects=True, vmem_limit_bytes=56 * 1024 * 1024),
        name="exchange",
    )(grads_out, inputs, basis_out, basis_in, lengths)
    return pl.pallas_call(
        functools.partial(square_kernel, n, length, 1.0 / rows),
        out_shape=jax.ShapeDtypeStruct((columns, panel_width), F32),
        grid=(nc,),
        in_specs=[
            pl.BlockSpec((1, rows, chunk), lambda i: (i, 0, 0)),
            pl.BlockSpec((rows, panel_width), lambda i: (0, 0)),
        ],
        out_specs=pl.BlockSpec((chunk, panel_width), lambda i: (i, 0)),
        cost_estimate=pl.CostEstimate(
            flops=2 * rows * columns * panel_width, bytes_accessed=4 * columns * panel_width, transcendentals=0),
        compiler_params=pltpu.CompilerParams(vmem_limit_bytes=48 * 1024 * 1024),
        name="square_sum",
    )(rotated, panel)


def solution(mesh):
    placed = (P("dp", None), P("dp", None), P("dp", "tensor"), P("tensor", "dp"), P("dp"))
    return jax.shard_map(
        per_device, mesh=mesh, in_specs=placed, out_specs=P("tensor", "dp"), check_vma=False
    )
```

```python
import functools

import jax
import jax.numpy as jnp
from jax import lax
from jax.experimental import pallas as pl
from jax.experimental.pallas import tpu as pltpu
from jax.sharding import PartitionSpec as P

MESH = pl.DeviceIdType.MESH
BF16 = jnp.bfloat16
F32 = jnp.float32


def ring_to_dp(q, n):
    return jnp.where(q < n // 2, 2 * q, 2 * (n - 1 - q) + 1)


def exchange_kernel(
    n, tn, nc, share_y,
    grads, inputs, basis_out, basis_in, lengths,
    summed_out, last_rotated, last_panel,
    gathered, basis, slab, basis_small, partial, early_send, early_recv, late_send, late_recv, rotated,
    panel_part, panel_recv, panel, summed,
    a_send, a_recv, fy_send, fy_recv, fc_send, fc_recv, fd_send, fd_recv,
    in_send, in_recv, rs_ssem, rs_rsem, ag_ssem, ag_rsem,
    pr_send, pr_recv, pg_send, pg_recv, local_sem,
):
    d = lax.axis_index("dp")
    t = lax.axis_index("tensor")
    half = n // 2
    length = grads.shape[0]
    hl = length // 2
    width = gathered.shape[1]
    chunk = partial.shape[1] // nc
    slab_width = slab.shape[1]
    z, x = d // 2, d % 2
    pos = jnp.where(x == 0, z, n - 1 - z)
    core = t % 2
    up = t // 2

    def at_ring(offset):
        return ring_to_dp(lax.rem(pos + offset + 2 * n, n), n)

    def rows_of(index, extra=0, size=length):
        return pl.ds(pl.multiple_of(index * length + extra, hl), size)

    basis_copies = []
    pieces = 4
    step_rows = width // pieces
    for i in range(pieces):
        r = pl.ds(i * step_rows, step_rows)
        basis_copies.append(pltpu.make_async_copy(basis_out.at[r], basis.at[r], local_sem.at[i]))
    own_cols = pl.ds(pl.multiple_of(d * width, 128), width)
    own_grads = pltpu.make_async_copy(grads.at[:, own_cols], gathered.at[rows_of(d)], local_sem.at[pieces])
    slab_cols = pl.ds(pl.multiple_of(t * slab_width, 128), slab_width)
    own_slab = pltpu.make_async_copy(inputs.at[:, slab_cols], slab.at[rows_of(d)], local_sem.at[pieces + 1])
    own_small = pltpu.make_async_copy(basis_in, basis_small, local_sem.at[pieces + 2])
    own_grads.start()
    own_slab.start()
    for c in basis_copies:
        c.start()
    own_small.start()

    barrier = pltpu.get_barrier_semaphore()
    for k in range(1, n):
        pl.semaphore_signal(barrier, inc=1, device_id=(lax.rem(d + k, n), t), device_id_type=MESH)
    for k in range(1, tn):
        pl.semaphore_signal(barrier, inc=1, device_id=(d, lax.rem(t + k, tn)), device_id_type=MESH)
    pl.semaphore_wait(barrier, n - 1 + tn - 1)

    piece = width // share_y
    my_y = up if share_y == 2 else 0
    row_extra = core * hl
    mine = pl.ds(pl.multiple_of(my_y * piece, 128), piece)
    other = pl.ds(pl.multiple_of((1 - my_y) * piece, 128), piece)

    def a_copy(k, source, target):
        cols = pl.ds(pl.multiple_of(target * width + my_y * piece, 128), piece)
        return pltpu.make_async_remote_copy(
            src_ref=grads.at[pl.ds(pl.multiple_of(row_extra, hl), hl), cols],
            dst_ref=gathered.at[rows_of(source, row_extra, hl), mine],
            send_sem=a_send.at[k], recv_sem=a_recv.at[k],
            device_id=(target, t), device_id_type=MESH)

    def forward(k, extra, cols, ssem, rsem, target_t):
        ref = gathered.at[rows_of(lax.rem(d - k + n, n), extra, hl), cols]
        return pltpu.make_async_remote_copy(
            src_ref=ref, dst_ref=ref, send_sem=ssem.at[k], recv_sem=rsem.at[k],
            device_id=(d, target_t), device_id_type=MESH)

    partner = up * 2 + (1 - core)
    across = lax.rem(t + 2, tn)
    order = []
    for k in range(1, n // 2 + 1):
        order.append(k)
        if n - k != k:
            order.append(n - k)
    order = order[::-1]
    for k in order:
        a_copy(k, d, lax.rem(d + k, n)).start()

    def in_copy(direction, s, receiving):
        sign = 1 if direction == 0 else -1
        q = (-sign) * (s + 1 if receiving else s)
        last = s == half - 1
        extra = direction * hl if last else 0
        ref = slab.at[rows_of(at_ring(q), extra, hl if last else length)]
        return pltpu.make_async_remote_copy(
            src_ref=ref, dst_ref=ref, send_sem=in_send.at[direction, s], recv_sem=in_recv.at[direction, s],
            device_id=(at_ring(sign), t), device_id_type=MESH)

    own_slab.wait()
    for direction in range(2):
        in_copy(direction, 0, False).start()

    for k in order:
        a_copy(k, lax.rem(d - k + n, n), d).wait_recv()
        if share_y == 2:
            forward(k, row_extra, mine, fy_send, fy_recv, across).start()
        forward(k, row_extra, mine, fc_send, fc_recv, partner).start()
    there = hl - row_extra
    for k in order:
        forward(k, there, mine, fc_send, fc_recv, partner).wait_recv()
    own_grads.wait()
    for c in basis_copies:
        c.wait()

    def cols_of(c):
        return pl.ds(pl.multiple_of(c * chunk, 128), chunk)

    if share_y == 2:
        def pass_across(i):
            k = jnp.where(i % 2 == 1, half + (i + 1) // 2, half - i // 2)
            forward(k, row_extra, other, fy_send, fy_recv, across).wait_recv()
            forward(k, row_extra, other, fd_send, fd_recv, partner).start()

        def first_half(c):
            cols = cols_of(c)
            partial[:, cols] = jnp.dot(gathered[:, mine], basis[mine, cols], preferred_element_type=F32)

        if nc == n - 1:
            lax.fori_loop(0, nc, lambda i, u: (first_half(i), pass_across(i), u)[2], 0)
        else:
            lax.fori_loop(0, n - 1, lambda i, u: (pass_across(i), u)[1], 0)
            lax.fori_loop(0, nc, lambda i, u: (first_half(i), u)[1], 0)
        for k in order:
            forward(k, there, other, fd_send, fd_recv, partner).wait_recv()

    early = early_send.shape[1]

    def rs_send(direction, s, c):
        return early_send.at[direction, s, c] if s < early else late_send.at[direction, s - early, c]

    def rs_recv(direction, s, c):
        return early_recv.at[direction, s, c] if s < early else late_recv.at[direction, s - early, c]

    def rs_copy(direction, s, c):
        size = hl if s == 0 else length
        r = pl.ds(0, size)
        sign = 1 if direction == 0 else -1
        return pltpu.make_async_remote_copy(
            src_ref=rs_send(direction, s, c).at[r], dst_ref=rs_recv(direction, s, c).at[r],
            send_sem=rs_ssem.at[direction, s, c], recv_sem=rs_rsem.at[direction, s, c],
            device_id=(at_ring(sign), t), device_id_type=MESH)

    def rotate(c):
        cols = cols_of(c)
        if share_y == 2:
            partial[:, cols] += jnp.dot(gathered[:, other], basis[other, cols], preferred_element_type=F32)
        else:
            partial[:, cols] = jnp.dot(gathered[...], basis[:, cols], preferred_element_type=F32)
        target = at_ring(half)
        for direction in range(2):
            early_send[direction, 0, c, :hl] = partial[rows_of(target, direction * hl, hl), cols].astype(BF16)
            rs_copy(direction, 0, c).start()

    done = 0
    for s in range(1, half):
        until = max(done, min(nc, (2 * s) if nc > 2 else 1))
        if until > done:
            lax.fori_loop(done, until, lambda c, u: (rotate(c), u)[1], 0)
        done = until
        for direction in range(2):
            in_copy(direction, s - 1, True).wait_recv()
            in_copy(direction, s, False).start()
    if done < nc:
        lax.fori_loop(done, nc, lambda c, u: (rotate(c), u)[1], 0)

    for direction in range(2):
        in_copy(direction, half - 1, True).wait_recv()
    own_small.wait()
    panel_part[...] = jnp.dot(slab[...], basis_small[...], preferred_element_type=F32)
    share = panel_part.shape[0] // tn

    def share_rows(index):
        return pl.ds(pl.multiple_of(index * share, 16), share)

    def pr_copy(k):
        target = lax.rem(t + k, tn)
        return pltpu.make_async_remote_copy(
            src_ref=panel_part.at[share_rows(target)], dst_ref=panel_recv.at[k],
            send_sem=pr_send.at[k], recv_sem=pr_recv.at[k],
            device_id=(d, target), device_id_type=MESH)

    def pg_copy(k, source):
        ref = panel.at[share_rows(source)]
        return pltpu.make_async_remote_copy(
            src_ref=ref, dst_ref=ref, send_sem=pg_send.at[k], recv_sem=pg_recv.at[k],
            device_id=(d, lax.rem(t + k, tn)), device_id_type=MESH)

    for k in range(1, tn):
        pr_copy(k).start()

    for s in range(1, half):
        def reduce_step(c, u, s=s):
            cols = cols_of(c)
            for direction in range(2):
                sign = 1 if direction == 0 else -1
                target = at_ring(sign * (half - s))
                rs_copy(direction, s - 1, c).wait_recv()
                if s == 1:
                    near = slice(0, hl) if direction == 0 else slice(hl, length)
                    far = slice(hl, length) if direction == 0 else slice(0, hl)
                    near_at, far_at = direction * hl, (1 - direction) * hl
                    early_send[direction, s, c, near] = (
                        partial[rows_of(target, near_at, hl), cols]
                        + early_recv[direction, 0, c, :hl].astype(F32)).astype(BF16)
                    early_send[direction, s, c, far] = partial[rows_of(target, far_at, hl), cols].astype(BF16)
                else:
                    late_send[direction, s - early, c] = (
                        partial[rows_of(target), cols] + rs_recv(direction, s - 1, c)[...].astype(F32))
                rs_copy(direction, s, c).start()
            return u
        lax.fori_loop(0, nc, reduce_step, 0)
        if s == 1:
            total = panel_part[share_rows(t)]
            for k in range(1, tn):
                pr_copy(k).wait_recv()
                total = total + panel_recv[k]
            panel[share_rows(t)] = total.astype(BF16)
            for k in range(1, tn):
                pg_copy(k, t).start()

    def ag_copy(direction, s, c, receiving):
        sign = 1 if direction == 0 else -1
        q = (-sign) * (s + 1 if receiving else s)
        last = s == half - 1
        extra = direction * hl if last else 0
        ref = rotated.at[c, rows_of(at_ring(q), extra, hl if last else length)]
        return pltpu.make_async_remote_copy(
            src_ref=ref, dst_ref=ref, send_sem=ag_ssem.at[direction, s, c], recv_sem=ag_rsem.at[direction, s, c],
            device_id=(at_ring(sign), t), device_id_type=MESH)

    for k in range(1, tn):
        pg_copy(k, lax.rem(t - k + tn, tn)).wait_recv()

    def square(c, index):
        example = lax.dot_general(
            rotated[c, rows_of(index)], panel[rows_of(index)], (((0,), (0,)), ((), ())),
            preferred_element_type=F32)
        return example * example

    live = lax.broadcasted_iota(jnp.int32, (length, chunk), 0) < lengths[0]

    def finish(c, u):
        cols = cols_of(c)
        for direction in range(2):
            rs_copy(direction, half - 1, c).wait_recv()
        total = partial[rows_of(d), cols]
        total = total + rs_recv(0, half - 1, c)[...] + rs_recv(1, half - 1, c)[...]
        rotated[c, rows_of(d)] = jnp.where(live, total, 0.0).astype(BF16)
        for direction in range(2):
            ag_copy(direction, 0, c, False).start()
        summed[cols] = square(c, d)
        return u
    lax.fori_loop(0, nc, finish, 0)
    for s in range(1, half):
        def pass_on(c, u, s=s):
            for direction in range(2):
                ag_copy(direction, s - 1, c, True).wait_recv()
                ag_copy(direction, s, c, False).start()
            summed[cols_of(c)] += square(c, at_ring(-s)) + square(c, at_ring(s))
            return u
        lax.fori_loop(0, nc, pass_on, 0)

    summed_store = pltpu.make_async_copy(summed, summed_out, local_sem.at[pieces + 3])
    summed_store.start()
    last_rows = rows_of(at_ring(half))
    panel_store = pltpu.make_async_copy(panel.at[last_rows], last_panel, local_sem.at[pieces + 4])
    panel_store.start()

    def last_step(c, u):
        for direction in range(2):
            ag_copy(direction, half - 1, c, True).wait_recv()
        return u
    lax.fori_loop(0, nc, last_step, 0)
    rotated_store = pltpu.make_async_copy(rotated.at[:, last_rows], last_rotated, local_sem.at[pieces + 5])
    rotated_store.start()

    for k in order:
        a_copy(k, d, lax.rem(d + k, n)).wait_send()
        forward(k, row_extra, mine, fc_send, fc_recv, partner).wait_send()
        if share_y == 2:
            forward(k, row_extra, mine, fy_send, fy_recv, across).wait_send()
            forward(k, row_extra, other, fd_send, fd_recv, partner).wait_send()
    for s in range(half):
        for direction in range(2):
            in_copy(direction, s, False).wait_send()

        def sent(c, u, s=s):
            for direction in range(2):
                rs_copy(direction, s, c).wait_send()
                ag_copy(direction, s, c, False).wait_send()
            return u
        lax.fori_loop(0, nc, sent, 0)
    for k in range(1, tn):
        pr_copy(k).wait_send()
        pg_copy(k, t).wait_send()
    summed_store.wait()
    panel_store.wait()
    rotated_store.wait()


def finish_kernel(scale, summed, rotated, panel, out):
    example = lax.dot_general(
        rotated[0], panel[...], (((0,), (0,)), ((), ())), preferred_element_type=F32)
    out[...] = (summed[...] + example * example) * scale


def pick_chunk(width):
    for size in (512, 256, 128):
        if width % size == 0:
            return size
    return width


def per_device(grads_out, inputs, basis_out, basis_in, lengths):
    n, tn = lax.axis_size("dp"), lax.axis_size("tensor")
    length = grads_out.shape[0]
    rows = n * length
    width, columns = basis_out.shape
    slab_width, panel_width = basis_in.shape
    half = n // 2
    chunk = pick_chunk(columns) if n <= 8 else columns
    nc = columns // chunk
    share_y = 2 if tn == 4 and width % 256 == 0 else 1
    dma = pltpu.SemaphoreType.DMA
    anywhere = pl.BlockSpec(memory_space=pl.ANY)
    flops = 2 * rows * width * columns + 2 * rows * slab_width * panel_width
    summed, last_rotated, last_panel = pl.pallas_call(
        functools.partial(exchange_kernel, n, tn, nc, share_y),
        out_shape=(
            jax.ShapeDtypeStruct((columns, panel_width), F32),
            jax.ShapeDtypeStruct((nc, length, chunk), BF16),
            jax.ShapeDtypeStruct((length, panel_width), BF16),
        ),
        in_specs=[anywhere] * 4 + [pl.BlockSpec(memory_space=pltpu.SMEM)],
        out_specs=(anywhere, anywhere, anywhere),
        scratch_shapes=[
            pltpu.VMEM((rows, width), BF16),
            pltpu.VMEM((width, columns), BF16),
            pltpu.VMEM((rows, slab_width), BF16),
            pltpu.VMEM((slab_width, panel_width), BF16),
            pltpu.VMEM((rows, columns), F32),
            pltpu.VMEM((2, 2, nc, length, chunk), BF16),
            pltpu.VMEM((2, 2, nc, length, chunk), BF16),
            pltpu.VMEM((2, half - 2, nc, length, chunk), F32),
            pltpu.VMEM((2, half - 2, nc, length, chunk), F32),
            pltpu.VMEM((nc, rows, chunk), BF16),
            pltpu.VMEM((rows, panel_width), F32),
            pltpu.VMEM((tn, rows // tn, panel_width), F32),
            pltpu.VMEM((rows, panel_width), BF16),
            pltpu.VMEM((columns, panel_width), F32),
            dma((n,)), dma((n,)), dma((n,)), dma((n,)), dma((n,)), dma((n,)), dma((n,)), dma((n,)),
            dma((2, half)), dma((2, half)),
            dma((2, half, nc)), dma((2, half, nc)), dma((2, half, nc)), dma((2, half, nc)),
            dma((tn,)), dma((tn,)), dma((tn,)), dma((tn,)),
            dma((10,)),
        ],
        cost_estimate=pl.CostEstimate(
            flops=flops, bytes_accessed=2 * (width * columns + slab_width * panel_width), transcendentals=0),
        compiler_params=pltpu.CompilerParams(
            collective_id=0, has_side_effects=True, vmem_limit_bytes=60 * 1024 * 1024),
        name="exchange",
    )(grads_out, inputs, basis_out, basis_in, lengths)
    return pl.pallas_call(
        functools.partial(finish_kernel, 1.0 / rows),
        out_shape=jax.ShapeDtypeStruct((columns, panel_width), F32),
        grid=(nc,),
        in_specs=[
            pl.BlockSpec((chunk, panel_width), lambda i: (i, 0)),
            pl.BlockSpec((1, length, chunk), lambda i: (i, 0, 0)),
            pl.BlockSpec((length, panel_width), lambda i: (0, 0)),
        ],
        out_specs=pl.BlockSpec((chunk, panel_width), lambda i: (i, 0)),
        cost_estimate=pl.CostEstimate(
            flops=2 * length * columns * panel_width, bytes_accessed=8 * columns * panel_width, transcendentals=0),
        compiler_params=pltpu.CompilerParams(vmem_limit_bytes=60 * 1024 * 1024),
        name="finish",
    )(summed, last_rotated, last_panel)


def solution(mesh):
    placed = (P("dp", None), P("dp", None), P("dp", "tensor"), P("tensor", "dp"), P("dp"))
    return jax.shard_map(
        per_device, mesh=mesh, in_specs=placed, out_specs=P("tensor", "dp"), check_vma=False
    )
```

```python
import functools

import jax
import jax.numpy as jnp
from jax import lax
from jax.experimental import pallas as pl
from jax.experimental.pallas import tpu as pltpu
from jax.sharding import PartitionSpec as P

MESH = pl.DeviceIdType.MESH
BF16 = jnp.bfloat16
F32 = jnp.float32


def ring_to_dp(q, n):
    return jnp.where(q < n // 2, 2 * q, 2 * (n - 1 - q) + 1)


def exchange_kernel(
    n, tn, nc, share_y,
    grads, inputs, basis_out, basis_in, lengths,
    summed_out, last_rotated, last_panel,
    gathered, basis, slab, basis_small, partial, early_send, early_recv, late_send, late_recv, rotated,
    panel_part, panel_recv, panel, summed,
    a_send, a_recv, fy_send, fy_recv, fc_send, fc_recv, fd_send, fd_recv,
    in_send, in_recv, rs_ssem, rs_rsem, ag_ssem, ag_rsem,
    pr_send, pr_recv, pg_send, pg_recv, local_sem,
):
    d = lax.axis_index("dp")
    t = lax.axis_index("tensor")
    half = n // 2
    length = grads.shape[0]
    hl = length // 2
    width = gathered.shape[1]
    chunk = partial.shape[1] // nc
    slab_width = slab.shape[1]
    z, x = d // 2, d % 2
    pos = jnp.where(x == 0, z, n - 1 - z)
    core = t % 2
    up = t // 2

    def at_ring(offset):
        return ring_to_dp(lax.rem(pos + offset + 2 * n, n), n)

    def rows_of(index, extra=0, size=length):
        return pl.ds(pl.multiple_of(index * length + extra, hl), size)

    basis_copies = []
    pieces = 4
    step_rows = width // pieces
    for i in range(pieces):
        r = pl.ds(i * step_rows, step_rows)
        basis_copies.append(pltpu.make_async_copy(basis_out.at[r], basis.at[r], local_sem.at[i]))
    own_cols = pl.ds(pl.multiple_of(d * width, 128), width)
    own_grads = pltpu.make_async_copy(grads.at[:, own_cols], gathered.at[rows_of(d)], local_sem.at[pieces])
    slab_cols = pl.ds(pl.multiple_of(t * slab_width, 128), slab_width)
    own_slab = pltpu.make_async_copy(inputs.at[:, slab_cols], slab.at[rows_of(d)], local_sem.at[pieces + 1])
    own_small = pltpu.make_async_copy(basis_in, basis_small, local_sem.at[pieces + 2])
    own_grads.start()
    own_slab.start()
    for c in basis_copies:
        c.start()
    own_small.start()

    barrier = pltpu.get_barrier_semaphore()
    for k in range(1, n):
        pl.semaphore_signal(barrier, inc=1, device_id=(lax.rem(d + k, n), t), device_id_type=MESH)
    for k in range(1, tn):
        pl.semaphore_signal(barrier, inc=1, device_id=(d, lax.rem(t + k, tn)), device_id_type=MESH)
    pl.semaphore_wait(barrier, n - 1 + tn - 1)

    piece = width // share_y
    my_y = up if share_y == 2 else 0
    row_extra = core * hl
    mine = pl.ds(pl.multiple_of(my_y * piece, 128), piece)
    other = pl.ds(pl.multiple_of((1 - my_y) * piece, 128), piece)

    def a_copy(k, source, target):
        cols = pl.ds(pl.multiple_of(target * width + my_y * piece, 128), piece)
        return pltpu.make_async_remote_copy(
            src_ref=grads.at[pl.ds(pl.multiple_of(row_extra, hl), hl), cols],
            dst_ref=gathered.at[rows_of(source, row_extra, hl), mine],
            send_sem=a_send.at[k], recv_sem=a_recv.at[k],
            device_id=(target, t), device_id_type=MESH)

    def forward(k, extra, cols, ssem, rsem, target_t):
        ref = gathered.at[rows_of(lax.rem(d - k + n, n), extra, hl), cols]
        return pltpu.make_async_remote_copy(
            src_ref=ref, dst_ref=ref, send_sem=ssem.at[k], recv_sem=rsem.at[k],
            device_id=(d, target_t), device_id_type=MESH)

    partner = up * 2 + (1 - core)
    across = lax.rem(t + 2, tn)
    order = []
    for k in range(1, n // 2 + 1):
        order.append(k)
        if n - k != k:
            order.append(n - k)
    order = order[::-1]
    for k in order:
        a_copy(k, d, lax.rem(d + k, n)).start()

    def in_copy(direction, s, receiving):
        sign = 1 if direction == 0 else -1
        q = (-sign) * (s + 1 if receiving else s)
        last = s == half - 1
        extra = direction * hl if last else 0
        ref = slab.at[rows_of(at_ring(q), extra, hl if last else length)]
        return pltpu.make_async_remote_copy(
            src_ref=ref, dst_ref=ref, send_sem=in_send.at[direction, s], recv_sem=in_recv.at[direction, s],
            device_id=(at_ring(sign), t), device_id_type=MESH)

    own_slab.wait()
    for direction in range(2):
        in_copy(direction, 0, False).start()

    for k in order:
        a_copy(k, lax.rem(d - k + n, n), d).wait_recv()
        if share_y == 2:
            forward(k, row_extra, mine, fy_send, fy_recv, across).start()
        forward(k, row_extra, mine, fc_send, fc_recv, partner).start()
    there = hl - row_extra
    for k in order:
        forward(k, there, mine, fc_send, fc_recv, partner).wait_recv()
    own_grads.wait()
    for c in basis_copies:
        c.wait()

    def cols_of(c):
        return pl.ds(pl.multiple_of(c * chunk, 128), chunk)

    if share_y == 2:
        def pass_across(i):
            k = jnp.where(i % 2 == 1, half + (i + 1) // 2, half - i // 2)
            forward(k, row_extra, other, fy_send, fy_recv, across).wait_recv()
            forward(k, row_extra, other, fd_send, fd_recv, partner).start()

        def first_half(c):
            cols = cols_of(c)
            partial[:, cols] = jnp.dot(gathered[:, mine], basis[mine, cols], preferred_element_type=F32)

        if nc == n - 1:
            lax.fori_loop(0, nc, lambda i, u: (first_half(i), pass_across(i), u)[2], 0)
        else:
            lax.fori_loop(0, n - 1, lambda i, u: (pass_across(i), u)[1], 0)
            lax.fori_loop(0, nc, lambda i, u: (first_half(i), u)[1], 0)
        for k in order:
            forward(k, there, other, fd_send, fd_recv, partner).wait_recv()

    early = early_send.shape[1]

    def rs_send(direction, s, c):
        return early_send.at[direction, s, c] if s < early else late_send.at[direction, s - early, c]

    def rs_recv(direction, s, c):
        return early_recv.at[direction, s, c] if s < early else late_recv.at[direction, s - early, c]

    def rs_copy(direction, s, c):
        size = hl if s == 0 else length
        r = pl.ds(0, size)
        sign = 1 if direction == 0 else -1
        return pltpu.make_async_remote_copy(
            src_ref=rs_send(direction, s, c).at[r], dst_ref=rs_recv(direction, s, c).at[r],
            send_sem=rs_ssem.at[direction, s, c], recv_sem=rs_rsem.at[direction, s, c],
            device_id=(at_ring(sign), t), device_id_type=MESH)

    def rotate(c):
        cols = cols_of(c)
        if share_y == 2:
            partial[:, cols] += jnp.dot(gathered[:, other], basis[other, cols], preferred_element_type=F32)
        else:
            partial[:, cols] = jnp.dot(gathered[...], basis[:, cols], preferred_element_type=F32)
        target = at_ring(half)
        for direction in range(2):
            early_send[direction, 0, c, :hl] = partial[rows_of(target, direction * hl, hl), cols].astype(BF16)
            rs_copy(direction, 0, c).start()

    done = 0
    for s in range(1, half):
        until = max(done, min(nc, (2 * s) if nc > 2 else 1))
        if until > done:
            lax.fori_loop(done, until, lambda c, u: (rotate(c), u)[1], 0)
        done = until
        for direction in range(2):
            in_copy(direction, s - 1, True).wait_recv()
            in_copy(direction, s, False).start()
    if done < nc:
        lax.fori_loop(done, nc, lambda c, u: (rotate(c), u)[1], 0)

    share = panel_part.shape[0] // tn

    def share_rows(index):
        return pl.ds(pl.multiple_of(index * share, 16), share)

    def pr_copy(k):
        target = lax.rem(t + k, tn)
        return pltpu.make_async_remote_copy(
            src_ref=panel_part.at[share_rows(target)], dst_ref=panel_recv.at[k],
            send_sem=pr_send.at[k], recv_sem=pr_recv.at[k],
            device_id=(d, target), device_id_type=MESH)

    def pg_copy(k, source):
        ref = panel.at[share_rows(source)]
        return pltpu.make_async_remote_copy(
            src_ref=ref, dst_ref=ref, send_sem=pg_send.at[k], recv_sem=pg_recv.at[k],
            device_id=(d, lax.rem(t + k, tn)), device_id_type=MESH)

    for s in range(1, half):
        def reduce_step(c, u, s=s):
            cols = cols_of(c)
            for direction in range(2):
                sign = 1 if direction == 0 else -1
                target = at_ring(sign * (half - s))
                rs_copy(direction, s - 1, c).wait_recv()
                if s == 1:
                    near = slice(0, hl) if direction == 0 else slice(hl, length)
                    far = slice(hl, length) if direction == 0 else slice(0, hl)
                    near_at, far_at = direction * hl, (1 - direction) * hl
                    early_send[direction, s, c, near] = (
                        partial[rows_of(target, near_at, hl), cols]
                        + early_recv[direction, 0, c, :hl].astype(F32)).astype(BF16)
                    early_send[direction, s, c, far] = partial[rows_of(target, far_at, hl), cols].astype(BF16)
                else:
                    late_send[direction, s - early, c] = (
                        partial[rows_of(target), cols] + rs_recv(direction, s - 1, c)[...].astype(F32))
                rs_copy(direction, s, c).start()
            return u
        lax.fori_loop(0, nc, reduce_step, 0)
        if s == 1:
            for direction in range(2):
                in_copy(direction, half - 1, True).wait_recv()
            own_small.wait()
            panel_part[...] = jnp.dot(slab[...], basis_small[...], preferred_element_type=F32)
            for k in range(1, tn):
                pr_copy(k).start()
        if s == 2:
            total = panel_part[share_rows(t)]
            for k in range(1, tn):
                pr_copy(k).wait_recv()
                total = total + panel_recv[k]
            panel[share_rows(t)] = total.astype(BF16)
            for k in range(1, tn):
                pg_copy(k, t).start()

    def ag_copy(direction, s, c, receiving):
        sign = 1 if direction == 0 else -1
        q = (-sign) * (s + 1 if receiving else s)
        last = s == half - 1
        extra = direction * hl if last else 0
        ref = rotated.at[c, rows_of(at_ring(q), extra, hl if last else length)]
        return pltpu.make_async_remote_copy(
            src_ref=ref, dst_ref=ref, send_sem=ag_ssem.at[direction, s, c], recv_sem=ag_rsem.at[direction, s, c],
            device_id=(at_ring(sign), t), device_id_type=MESH)

    for k in range(1, tn):
        pg_copy(k, lax.rem(t - k + tn, tn)).wait_recv()

    def square(c, index):
        example = lax.dot_general(
            rotated[c, rows_of(index)], panel[rows_of(index)], (((0,), (0,)), ((), ())),
            preferred_element_type=F32)
        return example * example

    live = lax.broadcasted_iota(jnp.int32, (length, chunk), 0) < lengths[0]

    def finish(c, u):
        cols = cols_of(c)
        for direction in range(2):
            rs_copy(direction, half - 1, c).wait_recv()
        total = partial[rows_of(d), cols]
        total = total + rs_recv(0, half - 1, c)[...] + rs_recv(1, half - 1, c)[...]
        rotated[c, rows_of(d)] = jnp.where(live, total, 0.0).astype(BF16)
        for direction in range(2):
            ag_copy(direction, 0, c, False).start()
        summed[cols] = square(c, d)
        return u
    lax.fori_loop(0, nc, finish, 0)
    for s in range(1, half):
        def pass_on(c, u, s=s):
            for direction in range(2):
                ag_copy(direction, s - 1, c, True).wait_recv()
                ag_copy(direction, s, c, False).start()
            summed[cols_of(c)] += square(c, at_ring(-s)) + square(c, at_ring(s))
            return u
        lax.fori_loop(0, nc, pass_on, 0)

    summed_store = pltpu.make_async_copy(summed, summed_out, local_sem.at[pieces + 3])
    summed_store.start()
    last_rows = rows_of(at_ring(half))
    panel_store = pltpu.make_async_copy(panel.at[last_rows], last_panel, local_sem.at[pieces + 4])
    panel_store.start()

    def last_step(c, u):
        for direction in range(2):
            ag_copy(direction, half - 1, c, True).wait_recv()
        return u
    lax.fori_loop(0, nc, last_step, 0)
    rotated_store = pltpu.make_async_copy(rotated.at[:, last_rows], last_rotated, local_sem.at[pieces + 5])
    rotated_store.start()

    for k in order:
        a_copy(k, d, lax.rem(d + k, n)).wait_send()
        forward(k, row_extra, mine, fc_send, fc_recv, partner).wait_send()
        if share_y == 2:
            forward(k, row_extra, mine, fy_send, fy_recv, across).wait_send()
            forward(k, row_extra, other, fd_send, fd_recv, partner).wait_send()
    for s in range(half):
        for direction in range(2):
            in_copy(direction, s, False).wait_send()

        def sent(c, u, s=s):
            for direction in range(2):
                rs_copy(direction, s, c).wait_send()
                ag_copy(direction, s, c, False).wait_send()
            return u
        lax.fori_loop(0, nc, sent, 0)
    for k in range(1, tn):
        pr_copy(k).wait_send()
        pg_copy(k, t).wait_send()
    summed_store.wait()
    panel_store.wait()
    rotated_store.wait()


def finish_kernel(scale, summed, rotated, panel, out):
    example = lax.dot_general(
        rotated[0], panel[...], (((0,), (0,)), ((), ())), preferred_element_type=F32)
    out[...] = (summed[...] + example * example) * scale


def pick_chunk(width):
    for size in (512, 256, 128):
        if width % size == 0:
            return size
    return width


def per_device(grads_out, inputs, basis_out, basis_in, lengths):
    n, tn = lax.axis_size("dp"), lax.axis_size("tensor")
    length = grads_out.shape[0]
    rows = n * length
    width, columns = basis_out.shape
    slab_width, panel_width = basis_in.shape
    half = n // 2
    chunk = pick_chunk(columns) if n <= 8 else columns
    nc = columns // chunk
    share_y = 2 if tn == 4 and width % 256 == 0 else 1
    dma = pltpu.SemaphoreType.DMA
    anywhere = pl.BlockSpec(memory_space=pl.ANY)
    flops = 2 * rows * width * columns + 2 * rows * slab_width * panel_width
    summed, last_rotated, last_panel = pl.pallas_call(
        functools.partial(exchange_kernel, n, tn, nc, share_y),
        out_shape=(
            jax.ShapeDtypeStruct((columns, panel_width), F32),
            jax.ShapeDtypeStruct((nc, length, chunk), BF16),
            jax.ShapeDtypeStruct((length, panel_width), BF16),
        ),
        in_specs=[anywhere] * 4 + [pl.BlockSpec(memory_space=pltpu.SMEM)],
        out_specs=(anywhere, anywhere, anywhere),
        scratch_shapes=[
            pltpu.VMEM((rows, width), BF16),
            pltpu.VMEM((width, columns), BF16),
            pltpu.VMEM((rows, slab_width), BF16),
            pltpu.VMEM((slab_width, panel_width), BF16),
            pltpu.VMEM((rows, columns), F32),
            pltpu.VMEM((2, 2, nc, length, chunk), BF16),
            pltpu.VMEM((2, 2, nc, length, chunk), BF16),
            pltpu.VMEM((2, half - 2, nc, length, chunk), F32),
            pltpu.VMEM((2, half - 2, nc, length, chunk), F32),
            pltpu.VMEM((nc, rows, chunk), BF16),
            pltpu.VMEM((rows, panel_width), F32),
            pltpu.VMEM((tn, rows // tn, panel_width), F32),
            pltpu.VMEM((rows, panel_width), BF16),
            pltpu.VMEM((columns, panel_width), F32),
            dma((n,)), dma((n,)), dma((n,)), dma((n,)), dma((n,)), dma((n,)), dma((n,)), dma((n,)),
            dma((2, half)), dma((2, half)),
            dma((2, half, nc)), dma((2, half, nc)), dma((2, half, nc)), dma((2, half, nc)),
            dma((tn,)), dma((tn,)), dma((tn,)), dma((tn,)),
            dma((10,)),
        ],
        cost_estimate=pl.CostEstimate(
            flops=flops, bytes_accessed=2 * (width * columns + slab_width * panel_width), transcendentals=0),
        compiler_params=pltpu.CompilerParams(
            collective_id=0, has_side_effects=True, vmem_limit_bytes=60 * 1024 * 1024),
        name="exchange",
    )(grads_out, inputs, basis_out, basis_in, lengths)
    return pl.pallas_call(
        functools.partial(finish_kernel, 1.0 / rows),
        out_shape=jax.ShapeDtypeStruct((columns, panel_width), F32),
        grid=(nc,),
        in_specs=[
            pl.BlockSpec((chunk, panel_width), lambda i: (i, 0)),
            pl.BlockSpec((1, length, chunk), lambda i: (i, 0, 0)),
            pl.BlockSpec((length, panel_width), lambda i: (0, 0)),
        ],
        out_specs=pl.BlockSpec((chunk, panel_width), lambda i: (i, 0)),
        cost_estimate=pl.CostEstimate(
            flops=2 * length * columns * panel_width, bytes_accessed=8 * columns * panel_width, transcendentals=0),
        compiler_params=pltpu.CompilerParams(vmem_limit_bytes=60 * 1024 * 1024),
        name="finish",
    )(summed, last_rotated, last_panel)


def solution(mesh):
    placed = (P("dp", None), P("dp", None), P("dp", "tensor"), P("tensor", "dp"), P("dp"))
    return jax.shard_map(
        per_device, mesh=mesh, in_specs=placed, out_specs=P("tensor", "dp"), check_vma=False
    )
```
